256 devices in a mesh: loop: 8 (over x_hi, y), dp: 32 (over z, x_lo, core).
Axes of the slice: x: 4 (x_hi: 2, x_lo: 2; x = x_hi * 2 + x_lo), y: 4, z: 8, core: 2. Of those that a mesh axis runs over, the one named last changes fastest.
Arguments:
- inputs0: bfloat16 [8, 32, 4, 8, 4, 384], P('loop', 'dp'), may hold values from -6 to 6
- inputs1: bfloat16 [8, 32, 4, 8, 4, 384], P('loop', 'dp'), may hold values from -6 to 6
- cotan0: bfloat16 [8, 32, 4, 8, 4, 384], P('loop', 'dp'), may hold values from -6 to 6
- down_weight: bfloat16 [8, 10368, 384], P('loop', 'dp'), may hold values from -0.0625 to 0.0625
- up_weight: bfloat16 [8, 10368, 384], P('loop', 'dp'), may hold values from -0.0625 to 0.0625
Outputs:
- input_grad1: bfloat16 [8, 32, 4, 8, 4, 384], P('loop', 'dp')
- down_grad: float32 [8, 10368, 384], P('loop', 'dp')
- up_grad: float32 [8, 10368, 384], P('loop', 'dp')
The draws below stay inside these ranges and needn't reach their ends.
All inputs are finite; a program needn't handle non-finite values.
Results may differ from the reference program's by a relative error of at most 0.023.
Values may be sent and summed in bfloat16 or wider, within the bound.
No kernel may reach another device: no remote copies, remote signals or barrier semaphores. Data moves between devices by JAX's collectives and lax.ppermute only.
A program may use at most 128 MiB of HBM per device.

```python
import jax
import jax.numpy as jnp
from jax import lax

C = 384
SX = 4
SY = 8
SZ = 4
B_DEV = 1
SECTIONS = 8
BATCH = 32
N_DP = 32


def block_scale(own_key, dims, pieces, low, largest):
    level, own = 1.0, jax.random.fold_in(own_key, 6)
    for axis_at, blocks in pieces:
        draws = jnp.exp(jax.random.uniform(jax.random.fold_in(own, axis_at), (blocks,), jnp.float32, low / len(pieces), largest / len(pieces)))
        level = level * jnp.repeat(draws, dims[axis_at] // blocks).reshape([-1 if axis == axis_at else 1 for axis in range(len(dims))])
    return level


def normal_values(rng, shape, deviation, limit, shards=(), held_as=jnp.bfloat16):
    values = deviation * jax.random.normal(rng, shape, jnp.float32)
    if shards:
        values = values * block_scale(rng, shape, shards, -0.22, 0.18)
    return jnp.clip(values, -limit, limit).astype(held_as)


def setup_inputs(seed: int = 0) -> dict:
    arg_keys = jax.random.split(jax.random.key(seed), 6)
    inputs0 = normal_values(arg_keys[0], (SECTIONS, BATCH, SX, SY, SZ, C), 1.0, 6.0, ((0, 8), (1, 32)))
    inputs1 = normal_values(arg_keys[1], (SECTIONS, BATCH, SX, SY, SZ, C), 1.0, 6.0, ((0, 8), (1, 32)))
    cotan0 = normal_values(arg_keys[2], (SECTIONS, BATCH, SX, SY, SZ, C), 1.0, 6.0, ((0, 8), (1, 32)))
    down_weight = normal_values(arg_keys[3], (SECTIONS, 27 * C, C), (27 * C) ** -0.5, 0.0625, ((0, 8), (1, 32)))
    up_weight = normal_values(arg_keys[4], (SECTIONS, 27 * C, C), (27 * C) ** -0.5, 0.0625, ((0, 8), (1, 32)))
    return dict(inputs0=inputs0, inputs1=inputs1, cotan0=cotan0, down_weight=down_weight, up_weight=up_weight)


def convolve(volume, kernel, stride):
    return lax.conv_general_dilated(volume, kernel, (stride, stride, stride), [(1, 1), (1, 1), (1, 1)], dimension_numbers=('NDHWC', 'DHWIO', 'NDHWC'), precision=lax.Precision.HIGHEST)

def as_kernel(weight):
    return weight.astype(jnp.float32).reshape(3, 3, 3, C, C)

def upsample(values):
    widened = jnp.repeat(jnp.repeat(jnp.repeat(values, 2, axis=1), 2, axis=2), 2, axis=3)
    return widened

def pool_sum(values):
    batch, size_x, size_y, size_z, width = values.shape
    shaped = values.reshape(batch, size_x // 2, 2, size_y // 2, 2, size_z // 2, 2, width)
    return lax.optimization_barrier(jnp.sum(shaped, axis=(2, 4, 6)))

def section_pass(volume, cotangent, down_weight, up_weight):
    volume_f = volume.astype(jnp.float32)
    down_kernel = as_kernel(down_weight)
    up_kernel = as_kernel(up_weight)
    hidden = convolve(volume_f, down_kernel, 2)
    active = jax.nn.silu(hidden).astype(jnp.bfloat16)
    widened = upsample(active).astype(jnp.float32)
    cot_f = cotangent.astype(jnp.float32)
    _, pull_up = jax.vjp(lambda values, kernel: convolve(values, kernel, 1), widened, up_kernel)
    grad_up_in, grad_up_kernel = pull_up(cot_f)
    grad_act = pool_sum(grad_up_in)
    sigma = jax.nn.sigmoid(hidden)
    grad_hidden = (grad_act * sigma * (1.0 + hidden * (1.0 - sigma))).astype(jnp.bfloat16)
    _, pull_down = jax.vjp(lambda values, kernel: convolve(values, kernel, 2), volume_f, down_kernel)
    grad_volume, grad_down_kernel = pull_down(grad_hidden.astype(jnp.float32))
    grad_input = (cot_f + grad_volume).astype(jnp.bfloat16)
    return (grad_input, grad_down_kernel.reshape(27 * C, C), grad_up_kernel.reshape(27 * C, C))

def reference(inputs0, inputs1, cotan0, down_weight, up_weight):
    first_grads = lax.map(lambda parts: section_pass(*parts)[0], (inputs0, cotan0, down_weight, up_weight))
    second_cots = jnp.roll(first_grads, -1, axis=0)
    scale = 1.0 / (2 * BATCH)

    def section_grads(parts):
        first_in, first_cot, second_in, second_cot, down_w, up_w = parts
        shaped = tuple((value.reshape((N_DP, B_DEV) + value.shape[1:]) for value in (first_in, first_cot, second_in, second_cot)))

        def group_step(carry, piece):
            in_a, cot_a, in_b, cot_b = piece
            _, down_a, up_a = section_pass(in_a, cot_a, down_w, up_w)
            grad_b, down_b, up_b = section_pass(in_b, cot_b, down_w, up_w)
            down_part = lax.optimization_barrier(((down_a + down_b) * scale).astype(jnp.bfloat16)).astype(jnp.float32)
            up_part = lax.optimization_barrier(((up_a + up_b) * scale).astype(jnp.bfloat16)).astype(jnp.float32)
            return ((carry[0] + down_part, carry[1] + up_part), grad_b)
        zeros = jnp.zeros((27 * C, C), jnp.float32)
        (down_total, up_total), grads = lax.scan(group_step, (zeros, zeros), shaped)
        return (grads.reshape((BATCH,) + grads.shape[2:]), down_total, up_total)
    input_grad1, down_grad, up_grad = lax.map(section_grads, (inputs0, cotan0, inputs1, second_cots, down_weight, up_weight))
    return (input_grad1, down_grad, up_grad)
```

```python
import functools

import jax
import jax.numpy as jnp
import numpy as np
from jax import lax
from jax.experimental import pallas as pl
from jax.experimental.pallas import tpu as pltpu
from jax.sharding import PartitionSpec as P

WIDTH = 384
CELLS = 128
HALF = 16
TAPS = 27
TAPS_PAD = 28
ROWS = 324
ROWS_PAD = 336
CUT = 176
RING = 8
QUAD = 4
BF16 = jnp.bfloat16
F32 = jnp.float32


def tap_matrices():
    taps = np.zeros((TAPS_PAD * HALF, CELLS), np.float32)
    pooled = np.zeros((TAPS_PAD * HALF, CELLS), np.float32)
    sizes, halves = (4, 8, 4), (2, 4, 2)
    for tap in range(TAPS):
        shift = (tap // 9, tap // 3 % 3, tap % 3)
        for cell in range(CELLS):
            at = (cell // 32, cell // 4 % 8, cell % 4)
            for low in range(HALF):
                coarse = (low // 8, low // 2 % 4, low % 2)
                row = tap * HALF + low
                if all(at[i] == 2 * coarse[i] + shift[i] - 1 for i in range(3)):
                    taps[row, cell] = 1
                if all(
                    0 <= at[i] + shift[i] - 1 < sizes[i]
                    and (at[i] + shift[i] - 1) // 2 == coarse[i]
                    for i in range(3)
                ):
                    pooled[row, cell] = 1
    return taps, pooled


def place_of(device, step):
    block = (((device >> 2) + step) & (RING - 1)) * QUAD + (device & (QUAD - 1))
    tap = (TAPS * block) >> 5
    row = ROWS * block - WIDTH * tap
    return tap, pl.multiple_of((row >> 4) << 4, 16)


def dot(left, right, over_left, over_right):
    return lax.dot_general(
        left, right, (((over_left,), (over_right,)), ((), ())), preferred_element_type=F32
    )


def spread_blocks(device, blocks, spread):
    spread[...] = jnp.zeros_like(spread)
    for step in range(RING):
        _, row = place_of(device, step)
        spread[step, pl.ds(row, ROWS_PAD), :] = blocks[step][...]


def taps_kernel(taps_ref, pooled_ref, own, by_core, by_x, by_both, cols_ref, pool_ref):
    for sample, ref in enumerate((own, by_core, by_x, by_both)):
        for kind in range(3):
            matrix = pooled_ref if kind == 2 else taps_ref
            values = dot(matrix[...], ref[kind], 1, 0).astype(BF16)
            values = values.reshape(TAPS_PAD, HALF, WIDTH)
            if kind == 2:
                pool_ref[:, pl.ds(sample * HALF, HALF), :] = values
            else:
                cols_ref[:, pl.ds((kind * QUAD + sample) * HALF, HALF), :] = values


def hidden_kernel(device_ref, cols_ref, *refs):
    blocks, out, spread = refs[:RING], refs[RING], refs[RING + 1]
    device = device_ref[0]
    spread_blocks(device, blocks, spread)
    total = jnp.zeros(out.shape, F32)
    for step in range(RING):
        tap, _ = place_of(device, step)
        for part in range(2):
            total += dot(cols_ref[tap + part], spread[step, pl.ds(part * WIDTH, WIDTH), :], 1, 0)
    out[...] = total


def act_grad(device, pool_ref, blocks, spread):
    spread_blocks(device, blocks, spread)
    total = jnp.zeros((QUAD * HALF, WIDTH), F32)
    for step in range(RING):
        tap, _ = place_of(device, step)
        for part in range(2):
            total += dot(pool_ref[tap + part], spread[step, pl.ds(part * WIDTH, WIDTH), :], 1, 1)
    return total


def first_act_kernel(device_ref, pool_ref, *refs):
    blocks, out, spread = refs[:RING], refs[RING], refs[RING + 1]
    out[...] = act_grad(device_ref[0], pool_ref, blocks, spread).astype(BF16)


def second_act_kernel(device_ref, pooled_ref, own, by_core, by_x, by_both, *refs):
    blocks, out, pool_ref, spread = refs[:RING], refs[RING], refs[RING + 1], refs[RING + 2]
    for sample, ref in enumerate((own, by_core, by_x, by_both)):
        values = dot(pooled_ref[...], ref[...], 1, 0).astype(BF16)
        pool_ref[:, pl.ds(sample * HALF, HALF), :] = values.reshape(TAPS_PAD, HALF, WIDTH)
    out[...] = act_grad(device_ref[0], pool_ref, blocks, spread).astype(BF16)


def quad_total(refs, first_row):
    pieces = []
    for sample in range(QUAD):
        piece = None
        for partner in range(QUAD):
            rows = pl.ds(first_row + (sample ^ partner) * HALF, HALF)
            term = refs[partner][rows, :].astype(F32)
            piece = term if piece is None else piece + term
        pieces.append(piece)
    return jnp.concatenate(pieces, axis=0)


def hidden_grad(hidden, grad):
    sigma = jax.nn.sigmoid(hidden)
    return (grad * sigma * (1.0 + hidden * (1.0 - sigma))).astype(BF16)


def input_grad(device, grads, fold_ref, blocks, spread, columns):
    spread_blocks(device, blocks, spread)
    columns[...] = jnp.zeros_like(columns)
    for step in range(RING):
        tap, _ = place_of(device, step)
        for part in range(2):
            values = dot(grads, spread[step, pl.ds(part * WIDTH, WIDTH), :], 1, 1).astype(BF16)
            for sample in range(QUAD):
                columns[sample, tap + part] = values[sample * HALF : (sample + 1) * HALF]
    return [
        dot(fold_ref[...], columns[sample].reshape(TAPS_PAD * HALF, WIDTH), 1, 0)
        for sample in range(QUAD)
    ]


def first_grad_kernel(device_ref, fold_ref, *refs):
    hidden, grad, blocks = refs[:4], refs[4:8], refs[8:16]
    grad_out, outs, spread, columns = refs[16], refs[17:21], refs[21], refs[22]
    grads = hidden_grad(quad_total(hidden, 0), quad_total(grad, 0))
    grad_out[...] = grads
    results = input_grad(device_ref[0], grads, fold_ref, blocks, spread, columns)
    for out, result in zip(outs, results):
        out[...] = result.astype(BF16)


def second_grad_kernel(device_ref, fold_ref, grads_ref, *refs):
    blocks, outs, spread, columns = refs[:8], refs[8:12], refs[12], refs[13]
    results = input_grad(device_ref[0], grads_ref[...], fold_ref, blocks, spread, columns)
    for out, result in zip(outs, results):
        out[...] = result.astype(BF16)


def put_rows(device, step, wide, outs, scale):
    _, row = place_of(device, step)
    if step == RING // 2:
        outs[step][...] = (wide[pl.ds(row, CUT), :] * scale).astype(BF16)
        outs[RING][...] = (wide[pl.ds(row + CUT, ROWS_PAD - CUT), :] * scale).astype(BF16)
    else:
        outs[step][...] = (wide[pl.ds(row, ROWS_PAD), :] * scale).astype(BF16)


def down_kernel(scale, device_ref, cols_ref, first_ref, *refs):
    hidden, grad, outs = refs[:4], refs[4:8], refs[8 : 8 + RING + 1]
    grad_out, wide = refs[9 + RING], refs[10 + RING]
    device = device_ref[0]
    second = hidden_grad(quad_total(hidden, QUAD * HALF), quad_total(grad, 0))
    grad_out[...] = second
    both = jnp.concatenate([first_ref[...], second], axis=0)
    for step in range(RING):
        tap, _ = place_of(device, step)
        for part in range(2):
            wide[step, pl.ds(part * WIDTH, WIDTH), :] = dot(cols_ref[tap + part], both, 0, 0)
        put_rows(device, step, wide.at[step], outs, scale)


def up_kernel(scale, device_ref, first_pool, second_pool, *refs):
    hidden, outs, wide = refs[:4], refs[4 : 4 + RING + 1], refs[5 + RING]
    device = device_ref[0]
    rows = QUAD * HALF
    total = jnp.concatenate([quad_total(hidden, 0), quad_total(hidden, rows)], axis=0)
    active = jax.nn.silu(total).astype(BF16)
    for step in range(RING):
        tap, _ = place_of(device, step)
        for part in range(2):
            pools = jnp.concatenate([first_pool[tap + part], second_pool[tap + part]], axis=0)
            wide[step, pl.ds(part * WIDTH, WIDTH), :] = dot(active, pools, 0, 0)
        put_rows(device, step, wide.at[step], outs, scale)


def call(kernel, outs, scratch, flops, *operands):
    in_vmem = pl.BlockSpec(memory_space=pltpu.VMEM)
    specs = [
        pl.BlockSpec(memory_space=pltpu.SMEM) if operand.dtype == jnp.int32 else in_vmem
        for operand in operands
    ]
    moved = sum(operand.size * 2 for operand in operands)
    return pl.pallas_call(
        kernel,
        out_shape=[jax.ShapeDtypeStruct(shape, dtype) for shape, dtype in outs],
        in_specs=specs,
        out_specs=[in_vmem] * len(outs),
        scratch_shapes=[pltpu.VMEM(shape, dtype) for shape, dtype in scratch],
        compiler_params=pltpu.CompilerParams(vmem_limit_bytes=36 * 1024 * 1024),
        cost_estimate=pl.CostEstimate(flops=flops, bytes_accessed=moved, transcendentals=0),
    )(*operands)


def from_partner(block, bits, devices):
    return lax.ppermute(block, "dp", [(i ^ bits, i) for i in range(devices)])


def from_quad(block, devices):
    return tuple(from_partner(block, bits, devices) for bits in (1, 2, 3))


def from_ring(block, ahead, devices):
    return lax.ppermute(block, "dp", [((i + QUAD * ahead) % devices, i) for i in range(devices)])


def ring_gather(block, devices):
    held = [None] * RING
    held[0] = up = down = block
    for step in range(1, RING // 2):
        held[step] = up = from_ring(up, 1, devices)
        held[RING - step] = down = from_ring(down, -1, devices)
    held[RING // 2] = jnp.concatenate(
        [from_ring(up[:CUT], 1, devices), from_ring(down[CUT:], -1, devices)], axis=0
    )
    return held


def added(left, right):
    return (left.astype(F32) + right.astype(F32)).astype(BF16)


def ring_reduce(blocks, devices):
    ahead = from_ring(blocks[RING // 2], -1, devices)
    behind = from_ring(blocks[RING], 1, devices)
    own = blocks[RING // 2 - 1]
    ahead = jnp.concatenate([added(own[:CUT], ahead), own[CUT:]], axis=0)
    own = blocks[RING // 2 + 1]
    behind = jnp.concatenate([own[:CUT], added(own[CUT:], behind)], axis=0)
    for step in range(RING // 2 - 1, 1, -1):
        ahead = added(from_ring(ahead, -1, devices), blocks[step - 1])
        behind = added(from_ring(behind, 1, devices), blocks[RING - step + 1])
    ahead = from_ring(ahead, -1, devices)
    behind = from_ring(behind, 1, devices)
    return blocks[0].astype(F32) + ahead.astype(F32) + behind.astype(F32)


def local(inputs0, inputs1, cotan0, down_weight, up_weight):
    devices = lax.axis_size("dp")
    sections = lax.axis_size("loop")
    index = lax.axis_index("dp")
    device = index.astype(jnp.int32).reshape(1)
    skew = (ROWS * index) % 16
    scale = 1.0 / (2 * devices)
    taps_np, pooled_np = tap_matrices()
    taps, pooled = jnp.asarray(taps_np, BF16), jnp.asarray(pooled_np, BF16)
    fold = jnp.asarray(taps_np.T, BF16)

    def aligned(weight):
        return lax.dynamic_update_slice(jnp.zeros((ROWS_PAD, WIDTH), BF16), weight[0], (skew, 0))

    cot0 = cotan0.reshape(CELLS, WIDTH)
    stacked = jnp.stack(
        [inputs0.reshape(CELLS, WIDTH), inputs1.reshape(CELLS, WIDTH), cot0], axis=0
    )
    quad_rows = QUAD * HALF
    spread = ((RING, 2 * WIDTH, WIDTH), BF16)
    columns = ((QUAD, TAPS_PAD, HALF, WIDTH), BF16)
    wide = ((RING, 2 * WIDTH, WIDTH), F32)
    pool_shape = ((TAPS_PAD, quad_rows, WIDTH), BF16)
    small = ((quad_rows, WIDTH), BF16)
    volume = ((CELLS, WIDTH), BF16)
    block_outs = [((CUT if k == RING // 2 else ROWS_PAD, WIDTH), BF16) for k in range(RING)]
    block_outs.append(((ROWS_PAD - CUT, WIDTH), BF16))
    work = 2 * quad_rows * 2 * RING * WIDTH * WIDTH

    down_blocks = ring_gather(aligned(down_weight), devices)
    up_blocks = ring_gather(aligned(up_weight), devices)
    cols, pool0 = call(
        taps_kernel,
        [((TAPS_PAD, 2 * quad_rows, WIDTH), BF16), pool_shape],
        [],
        work,
        taps,
        pooled,
        stacked,
        *from_quad(stacked, devices),
    )
    (hidden,) = call(
        hidden_kernel,
        [((2 * quad_rows, WIDTH), F32)],
        [spread],
        2 * work,
        device,
        cols,
        *down_blocks,
    )
    hiddens = (hidden,) + from_quad(hidden, devices)
    (act0,) = call(first_act_kernel, [small], [spread], work, device, pool0, *up_blocks)
    acts0 = (act0,) + from_quad(act0, devices)
    grads0, *partial = call(
        first_grad_kernel,
        [small] + [volume] * QUAD,
        [spread, columns],
        2 * work,
        device,
        fold,
        *hiddens,
        *acts0,
        *down_blocks,
    )

    def summed(partial, cotangent):
        total = cotangent.astype(F32) + partial[0].astype(F32)
        for bits in range(1, QUAD):
            total = total + from_partner(partial[bits], bits, devices).astype(F32)
        return total.astype(BF16)

    grad_in0 = summed(partial, cot0)
    cot1 = lax.ppermute(grad_in0, "loop", [((i + 1) % sections, i) for i in range(sections)])
    act1, pool1 = call(
        second_act_kernel,
        [small, pool_shape],
        [spread],
        2 * work,
        device,
        pooled,
        cot1,
        *from_quad(cot1, devices),
        *up_blocks,
    )
    acts1 = (act1,) + from_quad(act1, devices)
    up_parts = call(
        functools.partial(up_kernel, scale),
        block_outs,
        [wide],
        2 * work,
        device,
        pool0,
        pool1,
        *hiddens,
    )
    *down_parts, grads1 = call(
        functools.partial(down_kernel, scale),
        block_outs + [small],
        [wide],
        2 * work,
        device,
        cols,
        grads0,
        *hiddens,
        *acts1,
    )
    partial = call(
        second_grad_kernel,
        [volume] * QUAD,
        [spread, columns],
        2 * work,
        device,
        fold,
        grads1,
        *down_blocks,
    )
    grad_in1 = summed(partial, cot1)
    up_sum = ring_reduce(up_parts, devices)
    down_sum = ring_reduce(down_parts, devices)

    def owned(total):
        return lax.dynamic_slice(total, (skew, 0), (ROWS, WIDTH))[None]

    return (grad_in1.reshape(inputs1.shape), owned(down_sum), owned(up_sum))


def solution(mesh):
    volume = P("loop", "dp", None, None, None, None)
    rows = P("loop", "dp", None)
    return jax.shard_map(
        local,
        mesh=mesh,
        in_specs=(volume, volume, volume, rows, rows),
        out_specs=(volume, rows, rows),
        check_vma=False,
    )
```

```python
import functools

import jax
import jax.numpy as jnp
import numpy as np
from jax import lax
from jax.experimental import pallas as pl
from jax.experimental.pallas import tpu as pltpu
from jax.sharding import PartitionSpec as P

WIDTH = 384
CELLS = 128
HALF = 16
TAPS = 27
TAPS_PAD = 28
ROWS = 324
ROWS_PAD = 336
CUT = 176
RING = 8
QUAD = 4
LOTS = ((0, 1, 7), (2, 6), (3, 5, 4))
ADD_WORK = 4 * ROWS_PAD * WIDTH
BF16 = jnp.bfloat16
F32 = jnp.float32


class Idle:
    def __init__(self, array):
        self.array = array


def idle(*arrays):
    return [Idle(array) for array in arrays]


def tap_matrices():
    taps = np.zeros((TAPS_PAD * HALF, CELLS), np.float32)
    pooled = np.zeros((TAPS_PAD * HALF, CELLS), np.float32)
    sizes, halves = (4, 8, 4), (2, 4, 2)
    for tap in range(TAPS):
        shift = (tap // 9, tap // 3 % 3, tap % 3)
        for cell in range(CELLS):
            at = (cell // 32, cell // 4 % 8, cell % 4)
            for low in range(HALF):
                coarse = (low // 8, low // 2 % 4, low % 2)
                row = tap * HALF + low
                if all(at[i] == 2 * coarse[i] + shift[i] - 1 for i in range(3)):
                    taps[row, cell] = 1
                if all(
                    0 <= at[i] + shift[i] - 1 < sizes[i]
                    and (at[i] + shift[i] - 1) // 2 == coarse[i]
                    for i in range(3)
                ):
                    pooled[row, cell] = 1
    return taps, pooled


def place_of(device, step):
    block = (((device >> 2) + step) & (RING - 1)) * QUAD + (device & (QUAD - 1))
    tap = (TAPS * block) >> 5
    row = ROWS * block - WIDTH * tap
    return tap, pl.multiple_of((row >> 4) << 4, 16)


def dot(left, right, over_left, over_right):
    return lax.dot_general(
        left, right, (((over_left,), (over_right,)), ((), ())), preferred_element_type=F32
    )


def spread_blocks(device, lot, blocks, spread):
    spread[...] = jnp.zeros_like(spread)
    for at, step in enumerate(LOTS[lot]):
        _, row = place_of(device, step)
        pieces = [blocks[at]]
        if step == RING // 2:
            pieces.append(blocks[at + 1])
        for piece in pieces:
            rows = piece.shape[0]
            spread[at, pl.ds(row, rows), :] = piece[...]
            row = row + rows


def each_part(device, spreads):
    for lot, spread in zip(LOTS, spreads):
        for at, step in enumerate(lot):
            tap, _ = place_of(device, step)
            for part in range(2):
                yield tap + part, spread[at, pl.ds(part * WIDTH, WIDTH), :]


def spread_kernel(lot, device_ref, *refs):
    spread_blocks(device_ref[0], lot, refs[: len(LOTS[lot])], refs[-1])


def taps_kernel(
    taps_ref, pooled_ref, own, by_core, by_x, by_both, cols_ref, pool_ref, cot_ref
):
    cot_ref[...] = own[2]
    for sample, ref in enumerate((own, by_core, by_x, by_both)):
        for kind in range(3):
            matrix = pooled_ref if kind == 2 else taps_ref
            values = dot(matrix[...], ref[kind], 1, 0).astype(BF16)
            values = values.reshape(TAPS_PAD, HALF, WIDTH)
            if kind == 2:
                pool_ref[:, pl.ds(sample * HALF, HALF), :] = values
            else:
                cols_ref[:, pl.ds((kind * QUAD + sample) * HALF, HALF), :] = values


def hidden_kernel(device_ref, cols_ref, first, second, *refs):
    blocks, out, last = refs[:4], refs[-2], refs[-1]
    device = device_ref[0]
    spread_blocks(device, 2, blocks, last)
    total = jnp.zeros(out.shape, F32)
    for tap, weight in each_part(device, (first, second, last)):
        total += dot(cols_ref[tap], weight, 1, 0)
    out[...] = total.astype(BF16)


def act_grad(device, pool_ref, spreads):
    total = jnp.zeros((QUAD * HALF, WIDTH), F32)
    for tap, weight in each_part(device, spreads):
        total += dot(pool_ref[tap], weight, 1, 1)
    return total.astype(BF16)


def first_act_kernel(device_ref, pool_ref, first, second, *refs):
    blocks, out, last = refs[:4], refs[-2], refs[-1]
    device = device_ref[0]
    spread_blocks(device, 2, blocks, last)
    out[...] = act_grad(device, pool_ref, (first, second, last))


def second_act_kernel(device_ref, pooled_ref, *refs):
    sources, spreads, out, pool_ref = refs[:4], refs[4:7], refs[-2], refs[-1]
    for sample, ref in enumerate(sources):
        values = dot(pooled_ref[...], ref[...], 1, 0).astype(BF16)
        pool_ref[:, pl.ds(sample * HALF, HALF), :] = values.reshape(TAPS_PAD, HALF, WIDTH)
    out[...] = act_grad(device_ref[0], pool_ref, spreads)


def quad_total(refs, first_row):
    pieces = []
    for sample in range(QUAD):
        piece = None
        for partner in range(QUAD):
            rows = pl.ds(first_row + (sample ^ partner) * HALF, HALF)
            term = refs[partner][rows, :].astype(F32)
            piece = term if piece is None else piece + term
        pieces.append(piece)
    return jnp.concatenate(pieces, axis=0)


def hidden_grad(hidden, grad):
    sigma = jax.nn.sigmoid(hidden)
    return (grad * sigma * (1.0 + hidden * (1.0 - sigma))).astype(BF16)


def input_grad(device, grads, fold_ref, spreads, columns, outs):
    columns[...] = jnp.zeros_like(columns)
    for tap, weight in each_part(device, spreads):
        values = dot(grads, weight, 1, 1).astype(BF16)
        for sample in range(QUAD):
            columns[sample, tap] = values[sample * HALF : (sample + 1) * HALF]
    for sample in range(QUAD):
        taps = columns[sample].reshape(TAPS_PAD * HALF, WIDTH)
        outs[sample][...] = dot(fold_ref[...], taps, 1, 0).astype(BF16)


def first_grad_kernel(device_ref, fold_ref, *refs):
    hidden, grad, spreads = refs[:4], refs[4:8], refs[8:11]
    grad_out, outs, columns = refs[-6], refs[-5:-1], refs[-1]
    grads = hidden_grad(quad_total(hidden, 0), quad_total(grad, 0))
    grad_out[...] = grads
    input_grad(device_ref[0], grads, fold_ref, spreads, columns, outs)


def second_grad_kernel(device_ref, fold_ref, grads_ref, *refs):
    spreads, outs, columns = refs[:3], refs[-5:-1], refs[-1]
    input_grad(device_ref[0], grads_ref[...], fold_ref, spreads, columns, outs)


def sum_kernel(*refs):
    total = refs[0][...].astype(F32)
    for ref in refs[1:5]:
        total += ref[...].astype(F32)
    refs[-1][...] = total.astype(BF16)


def put_rows(device, step, wide, outs, scale):
    _, row = place_of(device, step)
    if step == RING // 2:
        outs[step][...] = (wide[pl.ds(row, CUT), :] * scale).astype(BF16)
        outs[RING][...] = (wide[pl.ds(row + CUT, ROWS_PAD - CUT), :] * scale).astype(BF16)
    else:
        outs[step][...] = (wide[pl.ds(row, ROWS_PAD), :] * scale).astype(BF16)


def down_kernel(scale, device_ref, cols_ref, first_ref, *refs):
    hidden, grad, outs = refs[:4], refs[4:8], refs[8 : 8 + RING + 1]
    grad_out, wide = refs[9 + RING], refs[10 + RING]
    device = device_ref[0]
    second = hidden_grad(quad_total(hidden, QUAD * HALF), quad_total(grad, 0))
    grad_out[...] = second
    both = jnp.concatenate([first_ref[...], second], axis=0)
    for step in range(RING):
        tap, _ = place_of(device, step)
        for part in range(2):
            wide[step % 2, pl.ds(part * WIDTH, WIDTH), :] = dot(cols_ref[tap + part], both, 0, 0)
        put_rows(device, step, wide.at[step % 2], outs, scale)


def up_kernel(scale, device_ref, first_pool, second_pool, *refs):
    hidden, outs, wide = refs[:4], refs[4 : 4 + RING + 1], refs[5 + RING]
    device = device_ref[0]
    rows = QUAD * HALF
    total = jnp.concatenate([quad_total(hidden, 0), quad_total(hidden, rows)], axis=0)
    active = jax.nn.silu(total).astype(BF16)
    for step in range(RING):
        tap, _ = place_of(device, step)
        for part in range(2):
            pools = jnp.concatenate([first_pool[tap + part], second_pool[tap + part]], axis=0)
            wide[step % 2, pl.ds(part * WIDTH, WIDTH), :] = dot(active, pools, 0, 0)
        put_rows(device, step, wide.at[step % 2], outs, scale)


def call(kernel, outs, scratch, flops, *operands):
    in_vmem = pl.BlockSpec(memory_space=pltpu.VMEM)

    def place(operand):
        if isinstance(operand, Idle):
            return pl.BlockSpec(memory_space=pl.ANY)
        if operand.dtype == jnp.int32:
            return pl.BlockSpec(memory_space=pltpu.SMEM)
        return in_vmem

    specs = [place(operand) for operand in operands]
    arrays = [o.array if isinstance(o, Idle) else o for o in operands]
    moved = sum(array.size * 2 for array in arrays)
    return pl.pallas_call(
        kernel,
        out_shape=[jax.ShapeDtypeStruct(shape, dtype) for shape, dtype in outs],
        in_specs=specs,
        out_specs=[in_vmem] * len(outs),
        scratch_shapes=[pltpu.VMEM(shape, dtype) for shape, dtype in scratch],
        compiler_params=pltpu.CompilerParams(vmem_limit_bytes=14 * 1024 * 1024),
        cost_estimate=pl.CostEstimate(flops=flops, bytes_accessed=moved, transcendentals=0),
    )(*arrays)


def from_partner(block, bits, devices):
    return lax.ppermute(block, "dp", [(i ^ bits, i) for i in range(devices)])


def from_quad(block, devices):
    return tuple(from_partner(block, bits, devices) for bits in (1, 2, 3))


def from_ring(block, ahead, devices):
    return lax.ppermute(block, "dp", [((i + QUAD * ahead) % devices, i) for i in range(devices)])


def ring_gather(block, devices):
    held = [None] * RING
    held[0] = up = down = block
    for step in range(1, RING // 2):
        held[step] = up = from_ring(up, 1, devices)
        held[RING - step] = down = from_ring(down, -1, devices)
    held[RING // 2] = from_ring(up[:CUT], 1, devices)
    return held + [from_ring(down[CUT:], -1, devices)]


def add_kernel(ahead, behind, own_ahead, own_behind, *refs):
    out_ahead, out_behind = refs[-2:]

    def added(out, own, got, first):
        rows = got.shape[0]
        if rows < ROWS_PAD:
            out[...] = own[...]
        total = own[pl.ds(first, rows), :].astype(F32) + got[...].astype(F32)
        out[pl.ds(first, rows), :] = total.astype(BF16)

    added(out_ahead, own_ahead, ahead, 0)
    added(out_behind, own_behind, behind, ROWS_PAD - behind.shape[0])


def add_and_finish_kernel(ahead, behind, own_ahead, own_behind, *refs):
    terms, outs = refs[:5], refs[-3:]
    add_kernel(ahead, behind, own_ahead, own_behind, *outs[:2])
    total = terms[0][...].astype(F32)
    for term in terms[1:]:
        total += term[...].astype(F32)
    outs[2][...] = total.astype(BF16)


def ring_reduce(blocks, devices, terms=()):
    ahead, behind = blocks[RING // 2], blocks[RING]
    block = ((ROWS_PAD, WIDTH), BF16)
    finished = None
    for step in range(RING // 2 - 1, -1, -1):
        ahead = from_ring(ahead, -1, devices)
        behind = from_ring(behind, 1, devices)
        if step:
            operands = (ahead, behind, blocks[step], blocks[RING - step])
            if terms and finished is None:
                outs = [block, block, ((CELLS, WIDTH), BF16)]
                ahead, behind, finished = call(
                    add_and_finish_kernel, outs, [], ADD_WORK, *operands, *terms, Idle(blocks[0])
                )
            else:
                ahead, behind = call(
                    add_kernel, [block, block], [], ADD_WORK, *operands, Idle(blocks[0])
                )
    total = blocks[0].astype(F32) + ahead.astype(F32) + behind.astype(F32)
    return total, finished


def local(inputs0, inputs1, cotan0, down_weight, up_weight):
    devices = lax.axis_size("dp")
    sections = lax.axis_size("loop")
    index = lax.axis_index("dp")
    device = index.astype(jnp.int32).reshape(1)
    skew = (ROWS * index) % 16
    scale = 1.0 / (2 * devices)
    taps_np, pooled_np = tap_matrices()
    taps, pooled = jnp.asarray(taps_np, BF16), jnp.asarray(pooled_np, BF16)
    fold = jnp.asarray(taps_np.T, BF16)

    def aligned(weight):
        return lax.dynamic_update_slice(jnp.zeros((ROWS_PAD, WIDTH), BF16), weight[0], (skew, 0))

    stacked = jnp.stack(
        [array.reshape(CELLS, WIDTH) for array in (inputs0, inputs1, cotan0)], axis=0
    )
    quad_rows = QUAD * HALF
    spread = [((len(lot), 2 * WIDTH, WIDTH), BF16) for lot in LOTS]
    columns = ((QUAD, TAPS_PAD, HALF, WIDTH), BF16)
    wide = ((2, 2 * WIDTH, WIDTH), F32)
    pool_shape = ((TAPS_PAD, quad_rows, WIDTH), BF16)
    small = ((quad_rows, WIDTH), BF16)
    volume = ((CELLS, WIDTH), BF16)
    block_outs = [((CUT if k == RING // 2 else ROWS_PAD, WIDTH), BF16) for k in range(RING)]
    block_outs.append(((ROWS_PAD - CUT, WIDTH), BF16))
    work = 2 * quad_rows * 2 * RING * WIDTH * WIDTH

    def lots(weight):
        blocks = ring_gather(aligned(weight), devices)
        early = [blocks[step] for step in LOTS[0]]
        (first,) = call(functools.partial(spread_kernel, 0), [spread[0]], [], 0, device, *early)
        middle = [blocks[step] for step in LOTS[1]]
        (second,) = call(
            functools.partial(spread_kernel, 1), [spread[1]], [], 0, device, *middle, Idle(first)
        )
        return first, second, blocks[3], blocks[5], blocks[4], blocks[RING]

    down_lots = lots(down_weight)
    up_lots = lots(up_weight)
    cols, pool0, cot0 = call(
        taps_kernel,
        [((TAPS_PAD, 2 * quad_rows, WIDTH), BF16), pool_shape, volume],
        [],
        work,
        taps,
        pooled,
        stacked,
        *from_quad(stacked, devices),
    )
    hidden, down_last = call(
        hidden_kernel,
        [((2 * quad_rows, WIDTH), BF16), spread[2]],
        [],
        2 * work,
        device,
        cols,
        *down_lots,
        *idle(cot0),
    )
    down_spread = (*down_lots[:2], down_last)
    hiddens = (hidden,) + from_quad(hidden, devices)
    act0, up_last = call(
        first_act_kernel,
        [small, spread[2]],
        [],
        work,
        device,
        pool0,
        *up_lots,
        *idle(cot0),
    )
    up_spread = (*up_lots[:2], up_last)
    acts0 = (act0,) + from_quad(act0, devices)
    grads0, *partial = call(
        first_grad_kernel,
        [small] + [volume] * QUAD,
        [columns],
        2 * work,
        device,
        fold,
        *hiddens,
        *acts0,
        *down_spread,
        *idle(cot0, pooled, *up_spread),
    )
    arrived = [from_partner(partial[bits], bits, devices) for bits in range(1, QUAD)]
    (grad_in0,) = call(
        sum_kernel,
        [volume],
        [],
        0,
        cot0,
        partial[0],
        *arrived,
        *idle(grads0, pooled, *up_spread, *down_spread, *hiddens),
    )
    cot1 = lax.ppermute(grad_in0, "loop", [((i + 1) % sections, i) for i in range(sections)])
    act1, pool1 = call(
        second_act_kernel,
        [small, pool_shape],
        [],
        2 * work,
        device,
        pooled,
        cot1,
        *from_quad(cot1, devices),
        *up_spread,
        *idle(grads0, *down_spread, *hiddens),
    )
    acts1 = (act1,) + from_quad(act1, devices)
    up_parts = call(
        functools.partial(up_kernel, scale),
        block_outs,
        [wide],
        2 * work,
        device,
        pool0,
        pool1,
        *hiddens,
    )
    *down_parts, grads1 = call(
        functools.partial(down_kernel, scale),
        block_outs + [small],
        [wide],
        2 * work,
        device,
        cols,
        grads0,
        *hiddens,
        *acts1,
    )
    partial = call(
        second_grad_kernel,
        [volume] * QUAD,
        [columns],
        2 * work,
        device,
        fold,
        grads1,
        *down_spread,
        *idle(up_parts[0], down_parts[0]),
    )
    arrived = [from_partner(partial[bits], bits, devices) for bits in range(1, QUAD)]
    up_sum, _ = ring_reduce(up_parts, devices)
    down_sum, grad_in1 = ring_reduce(down_parts, devices, (cot1, partial[0], *arrived))

    def owned(total):
        return lax.dynamic_slice(total, (skew, 0), (ROWS, WIDTH))[None]

    return (grad_in1.reshape(inputs1.shape), owned(down_sum), owned(up_sum))


def solution(mesh):
    volume = P("loop", "dp", None, None, None, None)
    rows = P("loop", "dp", None)
    return jax.shard_map(
        local,
        mesh=mesh,
        in_specs=(volume, volume, volume, rows, rows),
        out_specs=(volume, rows, rows),
        check_vma=False,
    )
```

```python
import functools

import jax
import jax.numpy as jnp
import numpy as np
from jax import lax
from jax.experimental import pallas as pl
from jax.experimental.pallas import tpu as pltpu
from jax.sharding import PartitionSpec as P

WIDTH = 384
CELLS = 128
HALF = 16
TAPS = 27
TAPS_PAD = 28
ROWS = 324
ROWS_PAD = 336
CUT = 176
RING = 8
QUAD = 4
LOTS = ((0, 1, 7), (2, 6), (3, 5, 4))
ADD_WORK = 4 * ROWS_PAD * WIDTH
BF16 = jnp.bfloat16
F32 = jnp.float32


class Idle:
    def __init__(self, array):
        self.array = array


def idle(*arrays):
    return [Idle(array) for array in arrays]


def tap_matrices():
    taps = np.zeros((TAPS_PAD * HALF, CELLS), np.float32)
    pooled = np.zeros((TAPS_PAD * HALF, CELLS), np.float32)
    sizes, halves = (4, 8, 4), (2, 4, 2)
    for tap in range(TAPS):
        shift = (tap // 9, tap // 3 % 3, tap % 3)
        for cell in range(CELLS):
            at = (cell // 32, cell // 4 % 8, cell % 4)
            for low in range(HALF):
                coarse = (low // 8, low // 2 % 4, low % 2)
                row = tap * HALF + low
                if all(at[i] == 2 * coarse[i] + shift[i] - 1 for i in range(3)):
                    taps[row, cell] = 1
                if all(
                    0 <= at[i] + shift[i] - 1 < sizes[i]
                    and (at[i] + shift[i] - 1) // 2 == coarse[i]
                    for i in range(3)
                ):
                    pooled[row, cell] = 1
    return taps, pooled


def place_of(device, step):
    block = (((device >> 2) + step) & (RING - 1)) * QUAD + (device & (QUAD - 1))
    tap = (TAPS * block) >> 5
    row = ROWS * block - WIDTH * tap
    return tap, pl.multiple_of((row >> 4) << 4, 16)


def dot(left, right, over_left, over_right):
    return lax.dot_general(
        left, right, (((over_left,), (over_right,)), ((), ())), preferred_element_type=F32
    )


def spread_blocks(device, lot, blocks, spread):
    spread[...] = jnp.zeros_like(spread)
    for at, step in enumerate(LOTS[lot]):
        _, row = place_of(device, step)
        pieces = [blocks[at]]
        if step == RING // 2:
            pieces.append(blocks[at + 1])
        for piece in pieces:
            rows = piece.shape[0]
            spread[at, pl.ds(row, rows), :] = piece[...]
            row = row + rows


def each_part(device, spreads):
    for lot, spread in zip(LOTS, spreads):
        for at, step in enumerate(lot):
            tap, _ = place_of(device, step)
            for part in range(2):
                yield tap + part, spread[at, pl.ds(part * WIDTH, WIDTH), :]


def spread_kernel(lot, device_ref, *refs):
    spread_blocks(device_ref[0], lot, refs[: len(LOTS[lot])], refs[-1])


def taps_kernel(
    taps_ref, pooled_ref, own, by_core, by_x, by_both, cols_ref, pool_ref, cot_ref
):
    cot_ref[...] = own[2]
    for sample, ref in enumerate((own, by_core, by_x, by_both)):
        for kind in range(3):
            matrix = pooled_ref if kind == 2 else taps_ref
            values = dot(matrix[...], ref[kind], 1, 0).astype(BF16)
            values = values.reshape(TAPS_PAD, HALF, WIDTH)
            if kind == 2:
                pool_ref[:, pl.ds(sample * HALF, HALF), :] = values
            else:
                cols_ref[:, pl.ds((kind * QUAD + sample) * HALF, HALF), :] = values


def hidden_kernel(device_ref, cols_ref, first, second, *refs):
    blocks, out, last = refs[:4], refs[-2], refs[-1]
    device = device_ref[0]
    spread_blocks(device, 2, blocks, last)
    total = jnp.zeros(out.shape, F32)
    for tap, weight in each_part(device, (first, second, last)):
        total += dot(cols_ref[tap], weight, 1, 0)
    out[...] = total.astype(BF16)


def act_grad(device, pool_ref, spreads):
    total = jnp.zeros((QUAD * HALF, WIDTH), F32)
    for tap, weight in each_part(device, spreads):
        total += dot(pool_ref[tap], weight, 1, 1)
    return total.astype(BF16)


def first_act_kernel(device_ref, pool_ref, first, second, *refs):
    blocks, out, last = refs[:4], refs[-2], refs[-1]
    device = device_ref[0]
    spread_blocks(device, 2, blocks, last)
    out[...] = act_grad(device, pool_ref, (first, second, last))


def second_act_kernel(device_ref, pooled_ref, *refs):
    sources, spreads, out, pool_ref = refs[:4], refs[4:7], refs[-2], refs[-1]
    for sample, ref in enumerate(sources):
        values = dot(pooled_ref[...], ref[...], 1, 0).astype(BF16)
        pool_ref[:, pl.ds(sample * HALF, HALF), :] = values.reshape(TAPS_PAD, HALF, WIDTH)
    out[...] = act_grad(device_ref[0], pool_ref, spreads)


def quad_total(refs, first_row):
    pieces = []
    for sample in range(QUAD):
        piece = None
        for partner in range(QUAD):
            rows = pl.ds(first_row + (sample ^ partner) * HALF, HALF)
            term = refs[partner][rows, :].astype(F32)
            piece = term if piece is None else piece + term
        pieces.append(piece)
    return jnp.concatenate(pieces, axis=0)


def hidden_grad(hidden, grad):
    sigma = jax.nn.sigmoid(hidden)
    return (grad * sigma * (1.0 + hidden * (1.0 - sigma))).astype(BF16)


def input_grad(device, grads, fold_ref, spreads, columns, outs):
    columns[...] = jnp.zeros_like(columns)
    for tap, weight in each_part(device, spreads):
        values = dot(grads, weight, 1, 1).astype(BF16)
        for sample in range(QUAD):
            columns[sample, tap] = values[sample * HALF : (sample + 1) * HALF]
    for sample in range(QUAD):
        taps = columns[sample].reshape(TAPS_PAD * HALF, WIDTH)
        outs[sample][...] = dot(fold_ref[...], taps, 1, 0).astype(BF16)


def first_grad_kernel(device_ref, fold_ref, *refs):
    hidden, grad, spreads = refs[:4], refs[4:8], refs[8:11]
    grad_out, outs, columns = refs[-6], refs[-5:-1], refs[-1]
    grads = hidden_grad(quad_total(hidden, 0), quad_total(grad, 0))
    grad_out[...] = grads
    input_grad(device_ref[0], grads, fold_ref, spreads, columns, outs)


def second_grad_kernel(device_ref, fold_ref, grads_ref, *refs):
    spreads, outs, columns = refs[:3], refs[-5:-1], refs[-1]
    input_grad(device_ref[0], grads_ref[...], fold_ref, spreads, columns, outs)


def sum_kernel(*refs):
    total = refs[0][...].astype(F32)
    for ref in refs[1:5]:
        total += ref[...].astype(F32)
    refs[-1][...] = total.astype(BF16)


def put_rows(device, step, wide, out, scale):
    _, row = place_of(device, step)
    out[...] = (wide[pl.ds(row, ROWS_PAD), :] * scale).astype(BF16)


def down_kernel(scale, device_ref, cols_ref, first_ref, *refs):
    hidden, grad, outs = refs[:4], refs[4:8], refs[8 : 8 + RING]
    grad_out, wide = refs[8 + RING], refs[9 + RING]
    device = device_ref[0]
    second = hidden_grad(quad_total(hidden, QUAD * HALF), quad_total(grad, 0))
    grad_out[...] = second
    both = jnp.concatenate([first_ref[...], second], axis=0)
    for step in range(RING):
        tap, _ = place_of(device, step)
        for part in range(2):
            wide[step % 2, pl.ds(part * WIDTH, WIDTH), :] = dot(cols_ref[tap + part], both, 0, 0)
        put_rows(device, step, wide.at[step % 2], outs[step], scale)


def up_kernel(scale, device_ref, first_pool, second_pool, *refs):
    hidden, outs, wide = refs[:4], refs[4 : 4 + RING], refs[4 + RING]
    device = device_ref[0]
    rows = QUAD * HALF
    total = jnp.concatenate([quad_total(hidden, 0), quad_total(hidden, rows)], axis=0)
    active = jax.nn.silu(total).astype(BF16)
    for step in range(RING):
        tap, _ = place_of(device, step)
        for part in range(2):
            pools = jnp.concatenate([first_pool[tap + part], second_pool[tap + part]], axis=0)
            wide[step % 2, pl.ds(part * WIDTH, WIDTH), :] = dot(active, pools, 0, 0)
        put_rows(device, step, wide.at[step % 2], outs[step], scale)


def call(kernel, outs, scratch, flops, *operands):
    in_vmem = pl.BlockSpec(memory_space=pltpu.VMEM)

    def place(operand):
        if isinstance(operand, Idle):
            return pl.BlockSpec(memory_space=pl.ANY)
        if operand.dtype == jnp.int32:
            return pl.BlockSpec(memory_space=pltpu.SMEM)
        return in_vmem

    specs = [place(operand) for operand in operands]
    arrays = [o.array if isinstance(o, Idle) else o for o in operands]
    moved = sum(array.size * 2 for array in arrays)
    return pl.pallas_call(
        kernel,
        out_shape=[jax.ShapeDtypeStruct(shape, dtype) for shape, dtype in outs],
        in_specs=specs,
        out_specs=[in_vmem] * len(outs),
        scratch_shapes=[pltpu.VMEM(shape, dtype) for shape, dtype in scratch],
        compiler_params=pltpu.CompilerParams(vmem_limit_bytes=14 * 1024 * 1024),
        cost_estimate=pl.CostEstimate(flops=flops, bytes_accessed=moved, transcendentals=0),
    )(*arrays)


def from_partner(block, bits, devices):
    return lax.ppermute(block, "dp", [(i ^ bits, i) for i in range(devices)])


def from_quad(block, devices):
    return tuple(from_partner(block, bits, devices) for bits in (1, 2, 3))


def from_ring(block, ahead, devices):
    return lax.ppermute(block, "dp", [((i + QUAD * ahead) % devices, i) for i in range(devices)])


def ring_gather(block, devices):
    held = [None] * RING
    held[0] = up = down = block
    for step in range(1, RING // 2):
        held[step] = up = from_ring(up, 1, devices)
        held[RING - step] = down = from_ring(down, -1, devices)
    held[RING // 2] = from_ring(up[:CUT], 1, devices)
    return held + [from_ring(down[CUT:], -1, devices)]


def from_quad_by_steps(block, devices):
    by_x = from_partner(block, 2, devices)
    return from_partner(block, 1, devices), by_x, from_partner(by_x, 1, devices)


def add_kernel(sides, *refs):
    gots, owns, outs = refs[:sides], refs[sides : 2 * sides], refs[-sides:]
    for got, own, out in zip(gots, owns, outs):
        out[...] = (own[...].astype(F32) + got[...].astype(F32)).astype(BF16)


def ring_reduce(blocks, far, devices, after=lambda mark: ()):
    block, near = ((ROWS_PAD, WIDTH), BF16), -far
    far_at, near_at = RING // 2, RING // 2 - 1
    far_sum, near_sum = blocks[far_at], blocks[near_at * near % RING]
    marks = []
    while near_at:
        far_sum = from_ring(far_sum, -far, devices)
        near_sum = from_ring(near_sum, -near, devices)
        far_at, near_at = far_at - 1, near_at - 1
        gots, owns, rest = [far_sum], [blocks[far_at * far % RING]], [blocks[0]]
        if near_at:
            gots.append(near_sum)
            owns.append(blocks[near_at * near % RING])
        else:
            rest.append(near_sum)
        sums = call(
            functools.partial(add_kernel, len(gots)),
            [block] * len(gots),
            [],
            ADD_WORK,
            *gots,
            *owns,
            *idle(*rest, *after(len(marks))),
        )
        far_sum = sums[0]
        if near_at:
            near_sum = sums[1]
        marks.append(far_sum)
    far_sum = from_ring(far_sum, -far, devices)
    return blocks[0].astype(F32) + far_sum.astype(F32) + near_sum.astype(F32), marks


def local(inputs0, inputs1, cotan0, down_weight, up_weight):
    devices = lax.axis_size("dp")
    sections = lax.axis_size("loop")
    index = lax.axis_index("dp")
    device = index.astype(jnp.int32).reshape(1)
    skew = (ROWS * index) % 16
    scale = 1.0 / (2 * devices)
    taps_np, pooled_np = tap_matrices()
    taps, pooled = jnp.asarray(taps_np, BF16), jnp.asarray(pooled_np, BF16)
    fold = jnp.asarray(taps_np.T, BF16)

    def aligned(weight):
        return lax.dynamic_update_slice(jnp.zeros((ROWS_PAD, WIDTH), BF16), weight[0], (skew, 0))

    stacked = jnp.stack(
        [array.reshape(CELLS, WIDTH) for array in (inputs0, inputs1, cotan0)], axis=0
    )
    quad_rows = QUAD * HALF
    spread = [((len(lot), 2 * WIDTH, WIDTH), BF16) for lot in LOTS]
    columns = ((QUAD, TAPS_PAD, HALF, WIDTH), BF16)
    wide = ((2, 2 * WIDTH, WIDTH), F32)
    pool_shape = ((TAPS_PAD, quad_rows, WIDTH), BF16)
    small = ((quad_rows, WIDTH), BF16)
    volume = ((CELLS, WIDTH), BF16)
    block_outs = [((ROWS_PAD, WIDTH), BF16)] * RING
    work = 2 * quad_rows * 2 * RING * WIDTH * WIDTH

    def lots(weight):
        blocks = ring_gather(aligned(weight), devices)
        early = [blocks[step] for step in LOTS[0]]
        (first,) = call(functools.partial(spread_kernel, 0), [spread[0]], [], 0, device, *early)
        middle = [blocks[step] for step in LOTS[1]]
        (second,) = call(
            functools.partial(spread_kernel, 1), [spread[1]], [], 0, device, *middle, Idle(first)
        )
        return first, second, blocks[3], blocks[5], blocks[4], blocks[RING]

    down_lots = lots(down_weight)
    up_lots = lots(up_weight)
    cols, pool0, cot0 = call(
        taps_kernel,
        [((TAPS_PAD, 2 * quad_rows, WIDTH), BF16), pool_shape, volume],
        [],
        work,
        taps,
        pooled,
        stacked,
        *from_quad(stacked, devices),
    )
    hidden, down_last = call(
        hidden_kernel,
        [((2 * quad_rows, WIDTH), BF16), spread[2]],
        [],
        2 * work,
        device,
        cols,
        *down_lots,
        *idle(cot0),
    )
    down_spread = (*down_lots[:2], down_last)
    hiddens = (hidden,) + from_quad(hidden, devices)
    act0, up_last = call(
        first_act_kernel,
        [small, spread[2]],
        [],
        work,
        device,
        pool0,
        *up_lots,
        *idle(cot0),
    )
    up_spread = (*up_lots[:2], up_last)
    acts0 = (act0,) + from_quad(act0, devices)
    grads0, *partial = call(
        first_grad_kernel,
        [small] + [volume] * QUAD,
        [columns],
        2 * work,
        device,
        fold,
        *hiddens,
        *acts0,
        *down_spread,
        *idle(cot0, pooled, *up_spread),
    )
    arrived = [from_partner(partial[bits], bits, devices) for bits in range(1, QUAD)]
    (grad_in0,) = call(
        sum_kernel,
        [volume],
        [],
        0,
        cot0,
        partial[0],
        *arrived,
        *idle(grads0, pooled, *up_spread, *down_spread, *hiddens),
    )
    cot1 = lax.ppermute(grad_in0, "loop", [((i + 1) % sections, i) for i in range(sections)])
    act1, pool1 = call(
        second_act_kernel,
        [small, pool_shape],
        [],
        2 * work,
        device,
        pooled,
        cot1,
        *from_quad_by_steps(cot1, devices),
        *up_spread,
        *idle(grads0, *down_spread, *hiddens),
    )
    acts1 = (act1,) + from_quad(act1, devices)
    up_parts = call(
        functools.partial(up_kernel, scale),
        block_outs,
        [wide],
        2 * work,
        device,
        pool0,
        pool1,
        *hiddens,
    )
    *down_parts, grads1 = call(
        functools.partial(down_kernel, scale),
        block_outs + [small],
        [wide],
        2 * work,
        device,
        cols,
        grads0,
        *hiddens,
        *acts1,
    )
    partial = call(
        second_grad_kernel,
        [volume] * QUAD,
        [columns],
        2 * work,
        device,
        fold,
        grads1,
        *down_spread,
    )
    arrived = [from_partner(partial[bits], bits, devices) for bits in range(1, QUAD)]
    (grad_in1,) = call(sum_kernel, [volume], [], 0, cot1, partial[0], *arrived)

    def after(ring):
        waits = {('down', 0): (partial[0],), ('up', 2): (grad_in1,)}
        return lambda mark: waits.get((ring, mark), ())

    up_sum, _ = ring_reduce(up_parts, -1, devices, after("up"))
    down_sum, _ = ring_reduce(down_parts, 1, devices, after("down"))

    def owned(total):
        return lax.dynamic_slice(total, (skew, 0), (ROWS, WIDTH))[None]

    return (grad_in1.reshape(inputs1.shape), owned(down_sum), owned(up_sum))


def solution(mesh):
    volume = P("loop", "dp", None, None, None, None)
    rows = P("loop", "dp", None)
    return jax.shard_map(
        local,
        mesh=mesh,
        in_specs=(volume, volume, volume, rows, rows),
        out_specs=(volume, rows, rows),
        check_vma=False,
    )
```

```python
import functools

import jax
import jax.numpy as jnp
import numpy as np
from jax import lax
from jax.experimental import pallas as pl
from jax.experimental.pallas import tpu as pltpu
from jax.sharding import PartitionSpec as P

WIDTH = 384
CELLS = 128
HALF = 16
TAPS = 27
TAPS_PAD = 28
ROWS = 324
ROWS_PAD = 336
CUT = 176
RING = 8
QUAD = 4
LOTS = ((0, 1, 7), (2, 6), (3, 5, 4))
ADD_WORK = 4 * ROWS_PAD * WIDTH
BF16 = jnp.bfloat16
F32 = jnp.float32


class Idle:
    def __init__(self, array):
        self.array = array


def idle(*arrays):
    return [Idle(array) for array in arrays]


def tap_matrices():
    taps = np.zeros((TAPS_PAD * HALF, CELLS), np.float32)
    pooled = np.zeros((TAPS_PAD * HALF, CELLS), np.float32)
    sizes, halves = (4, 8, 4), (2, 4, 2)
    for tap in range(TAPS):
        shift = (tap // 9, tap // 3 % 3, tap % 3)
        for cell in range(CELLS):
            at = (cell // 32, cell // 4 % 8, cell % 4)
            for low in range(HALF):
                coarse = (low // 8, low // 2 % 4, low % 2)
                row = tap * HALF + low
                if all(at[i] == 2 * coarse[i] + shift[i] - 1 for i in range(3)):
                    taps[row, cell] = 1
                if all(
                    0 <= at[i] + shift[i] - 1 < sizes[i]
                    and (at[i] + shift[i] - 1) // 2 == coarse[i]
                    for i in range(3)
                ):
                    pooled[row, cell] = 1
    return taps, pooled


def place_of(device, step):
    block = (((device >> 2) + step) & (RING - 1)) * QUAD + (device & (QUAD - 1))
    tap = (TAPS * block) >> 5
    row = ROWS * block - WIDTH * tap
    return tap, pl.multiple_of((row >> 4) << 4, 16)


def dot(left, right, over_left, over_right):
    return lax.dot_general(
        left, right, (((over_left,), (over_right,)), ((), ())), preferred_element_type=F32
    )


def spread_blocks(device, lot, blocks, spread):
    spread[...] = jnp.zeros_like(spread)
    for at, step in enumerate(LOTS[lot]):
        _, row = place_of(device, step)
        pieces = [blocks[at]]
        if step == RING // 2:
            pieces.append(blocks[at + 1])
        for piece in pieces:
            rows = piece.shape[0]
            spread[at, pl.ds(row, rows), :] = piece[...]
            row = row + rows


def each_part(device, spreads):
    for lot, spread in zip(LOTS, spreads):
        for at, step in enumerate(lot):
            tap, _ = place_of(device, step)
            for part in range(2):
                yield tap + part, spread[at, pl.ds(part * WIDTH, WIDTH), :]


def spread_kernel(lot, device_ref, *refs):
    spread_blocks(device_ref[0], lot, refs[: len(LOTS[lot])], refs[-1])


def taps_kernel(
    taps_ref, pooled_ref, own, by_core, by_x, by_both, cols_ref, pool_ref, cot_ref
):
    cot_ref[...] = own[2]
    for sample, ref in enumerate((own, by_core, by_x, by_both)):
        for kind in range(3):
            matrix = pooled_ref if kind == 2 else taps_ref
            values = dot(matrix[...], ref[kind], 1, 0).astype(BF16)
            values = values.reshape(TAPS_PAD, HALF, WIDTH)
            if kind == 2:
                pool_ref[:, pl.ds(sample * HALF, HALF), :] = values
            else:
                cols_ref[:, pl.ds((kind * QUAD + sample) * HALF, HALF), :] = values


def hidden_kernel(device_ref, cols_ref, first, second, *refs):
    blocks, out, last = refs[:4], refs[-2], refs[-1]
    device = device_ref[0]
    spread_blocks(device, 2, blocks, last)
    total = jnp.zeros(out.shape, F32)
    for tap, weight in each_part(device, (first, second, last)):
        total += dot(cols_ref[tap], weight, 1, 0)
    out[...] = total.astype(BF16)


def act_grad(device, pool_ref, spreads):
    total = jnp.zeros((QUAD * HALF, WIDTH), F32)
    for tap, weight in each_part(device, spreads):
        total += dot(pool_ref[tap], weight, 1, 1)
    return total.astype(BF16)


def first_act_kernel(device_ref, pool_ref, first, second, *refs):
    blocks, out, last = refs[:4], refs[-2], refs[-1]
    device = device_ref[0]
    spread_blocks(device, 2, blocks, last)
    out[...] = act_grad(device, pool_ref, (first, second, last))


def second_act_kernel(device_ref, pooled_ref, *refs):
    sources, spreads, out, pool_ref = refs[:4], refs[4:7], refs[-2], refs[-1]
    for sample, ref in enumerate(sources):
        values = dot(pooled_ref[...], ref[...], 1, 0).astype(BF16)
        pool_ref[:, pl.ds(sample * HALF, HALF), :] = values.reshape(TAPS_PAD, HALF, WIDTH)
    out[...] = act_grad(device_ref[0], pool_ref, spreads)


def quad_total(refs, first_row):
    pieces = []
    for sample in range(QUAD):
        piece = None
        for partner in range(QUAD):
            rows = pl.ds(first_row + (sample ^ partner) * HALF, HALF)
            term = refs[partner][rows, :].astype(F32)
            piece = term if piece is None else piece + term
        pieces.append(piece)
    return jnp.concatenate(pieces, axis=0)


def hidden_grad(hidden, grad):
    sigma = jax.nn.sigmoid(hidden)
    return (grad * sigma * (1.0 + hidden * (1.0 - sigma))).astype(BF16)


def input_grad(device, grads, fold_ref, spreads, columns, put):
    columns[...] = jnp.zeros_like(columns)
    for tap, weight in each_part(device, spreads):
        values = dot(grads, weight, 1, 1).astype(BF16)
        for sample in range(QUAD):
            columns[sample, tap] = values[sample * HALF : (sample + 1) * HALF]
    for sample in range(QUAD):
        taps = columns[sample].reshape(TAPS_PAD * HALF, WIDTH)
        put(sample, dot(fold_ref[...], taps, 1, 0).astype(BF16))


def first_grad_kernel(device_ref, fold_ref, *refs):
    hidden, grad, spreads = refs[:4], refs[4:8], refs[8:11]
    grad_out, outs, columns = refs[-6], refs[-5:-1], refs[-1]
    grads = hidden_grad(quad_total(hidden, 0), quad_total(grad, 0))
    grad_out[...] = grads

    def put(sample, value):
        outs[sample][...] = value

    input_grad(device_ref[0], grads, fold_ref, spreads, columns, put)


def second_grad_kernel(device_ref, fold_ref, grads_ref, *refs):
    spreads, outs, columns = refs[:3], refs[-3:-1], refs[-1]

    def put(sample, value):
        outs[sample & 1][pl.ds((sample >> 1) * CELLS, CELLS), :] = value

    input_grad(device_ref[0], grads_ref[...], fold_ref, spreads, columns, put)


def core_sum_kernel(kept, got, *refs):
    own, for_x = refs[-2:]
    total = kept[...].astype(F32) + got[...].astype(F32)
    own[...] = total[:CELLS]
    for_x[...] = total[CELLS:].astype(BF16)


def sum_kernel(terms, *refs):
    total = refs[0][...].astype(F32)
    for ref in refs[1:terms]:
        total += ref[...].astype(F32)
    refs[-1][...] = total.astype(BF16)


def put_rows(device, step, wide, out, scale):
    _, row = place_of(device, step)
    out[...] = (wide[pl.ds(row, ROWS_PAD), :] * scale).astype(BF16)


def down_kernel(scale, device_ref, cols_ref, first_ref, *refs):
    hidden, grad, outs = refs[:4], refs[4:8], refs[8 : 8 + RING]
    grad_out, wide = refs[8 + RING], refs[9 + RING]
    device = device_ref[0]
    second = hidden_grad(quad_total(hidden, QUAD * HALF), quad_total(grad, 0))
    grad_out[...] = second
    both = jnp.concatenate([first_ref[...], second], axis=0)
    for step in range(RING):
        tap, _ = place_of(device, step)
        for part in range(2):
            wide[step % 2, pl.ds(part * WIDTH, WIDTH), :] = dot(cols_ref[tap + part], both, 0, 0)
        put_rows(device, step, wide.at[step % 2], outs[step], scale)


def up_kernel(scale, device_ref, first_pool, second_pool, *refs):
    hidden, outs, wide = refs[:4], refs[4 : 4 + RING], refs[4 + RING]
    device = device_ref[0]
    rows = QUAD * HALF
    total = jnp.concatenate([quad_total(hidden, 0), quad_total(hidden, rows)], axis=0)
    active = jax.nn.silu(total).astype(BF16)
    for step in range(RING):
        tap, _ = place_of(device, step)
        for part in range(2):
            pools = jnp.concatenate([first_pool[tap + part], second_pool[tap + part]], axis=0)
            wide[step % 2, pl.ds(part * WIDTH, WIDTH), :] = dot(active, pools, 0, 0)
        put_rows(device, step, wide.at[step % 2], outs[step], scale)


def call(kernel, outs, scratch, flops, *operands):
    in_vmem = pl.BlockSpec(memory_space=pltpu.VMEM)

    def place(operand):
        if isinstance(operand, Idle):
            return pl.BlockSpec(memory_space=pl.ANY)
        if operand.dtype == jnp.int32:
            return pl.BlockSpec(memory_space=pltpu.SMEM)
        return in_vmem

    specs = [place(operand) for operand in operands]
    arrays = [o.array if isinstance(o, Idle) else o for o in operands]
    moved = sum(array.size * 2 for array in arrays)
    return pl.pallas_call(
        kernel,
        out_shape=[jax.ShapeDtypeStruct(shape, dtype) for shape, dtype in outs],
        in_specs=specs,
        out_specs=[in_vmem] * len(outs),
        scratch_shapes=[pltpu.VMEM(shape, dtype) for shape, dtype in scratch],
        compiler_params=pltpu.CompilerParams(vmem_limit_bytes=14 * 1024 * 1024),
        cost_estimate=pl.CostEstimate(flops=flops, bytes_accessed=moved, transcendentals=0),
    )(*arrays)


def from_partner(block, bits, devices):
    return lax.ppermute(block, "dp", [(i ^ bits, i) for i in range(devices)])


def from_quad(block, devices):
    return tuple(from_partner(block, bits, devices) for bits in (1, 2, 3))


def from_ring(block, ahead, devices):
    return lax.ppermute(block, "dp", [((i + QUAD * ahead) % devices, i) for i in range(devices)])


def ring_gather(block, devices):
    held = [None] * RING
    held[0] = up = down = block
    for step in range(1, RING // 2):
        held[step] = up = from_ring(up, 1, devices)
        held[RING - step] = down = from_ring(down, -1, devices)
    held[RING // 2] = from_ring(up[:CUT], 1, devices)
    return held + [from_ring(down[CUT:], -1, devices)]


def from_quad_by_steps(block, devices):
    by_x = from_partner(block, 2, devices)
    return from_partner(block, 1, devices), by_x, from_partner(by_x, 1, devices)


def add_kernel(sides, *refs):
    gots, owns, outs = refs[:sides], refs[sides : 2 * sides], refs[-sides:]
    for got, own, out in zip(gots, owns, outs):
        out[...] = (own[...].astype(F32) + got[...].astype(F32)).astype(BF16)


def ring_reduce(blocks, far, devices, after=lambda mark: ()):
    block, near = ((ROWS_PAD, WIDTH), BF16), -far
    far_at, near_at = RING // 2, RING // 2 - 1
    far_sum, near_sum = blocks[far_at], blocks[near_at * near % RING]
    marks = []
    while near_at:
        far_sum = from_ring(far_sum, -far, devices)
        near_sum = from_ring(near_sum, -near, devices)
        far_at, near_at = far_at - 1, near_at - 1
        gots, owns, rest = [far_sum], [blocks[far_at * far % RING]], [blocks[0]]
        if near_at:
            gots.append(near_sum)
            owns.append(blocks[near_at * near % RING])
        else:
            rest.append(near_sum)
        sums = call(
            functools.partial(add_kernel, len(gots)),
            [block] * len(gots),
            [],
            ADD_WORK,
            *gots,
            *owns,
            *idle(*rest, *after(len(marks))),
        )
        far_sum = sums[0]
        if near_at:
            near_sum = sums[1]
        marks.append(far_sum)
    far_sum = from_ring(far_sum, -far, devices)
    return blocks[0].astype(F32) + far_sum.astype(F32) + near_sum.astype(F32), marks


def local(inputs0, inputs1, cotan0, down_weight, up_weight):
    devices = lax.axis_size("dp")
    sections = lax.axis_size("loop")
    index = lax.axis_index("dp")
    device = index.astype(jnp.int32).reshape(1)
    skew = (ROWS * index) % 16
    scale = 1.0 / (2 * devices)
    taps_np, pooled_np = tap_matrices()
    taps, pooled = jnp.asarray(taps_np, BF16), jnp.asarray(pooled_np, BF16)
    fold = jnp.asarray(taps_np.T, BF16)

    def aligned(weight):
        return lax.dynamic_update_slice(jnp.zeros((ROWS_PAD, WIDTH), BF16), weight[0], (skew, 0))

    stacked = jnp.stack(
        [array.reshape(CELLS, WIDTH) for array in (inputs0, inputs1, cotan0)], axis=0
    )
    quad_rows = QUAD * HALF
    spread = [((len(lot), 2 * WIDTH, WIDTH), BF16) for lot in LOTS]
    columns = ((QUAD, TAPS_PAD, HALF, WIDTH), BF16)
    wide = ((2, 2 * WIDTH, WIDTH), F32)
    pool_shape = ((TAPS_PAD, quad_rows, WIDTH), BF16)
    small = ((quad_rows, WIDTH), BF16)
    volume = ((CELLS, WIDTH), BF16)
    block_outs = [((ROWS_PAD, WIDTH), BF16)] * RING
    work = 2 * quad_rows * 2 * RING * WIDTH * WIDTH

    def lots(weight):
        blocks = ring_gather(aligned(weight), devices)
        early = [blocks[step] for step in LOTS[0]]
        (first,) = call(functools.partial(spread_kernel, 0), [spread[0]], [], 0, device, *early)
        middle = [blocks[step] for step in LOTS[1]]
        (second,) = call(
            functools.partial(spread_kernel, 1), [spread[1]], [], 0, device, *middle, Idle(first)
        )
        return first, second, blocks[3], blocks[5], blocks[4], blocks[RING]

    down_lots = lots(down_weight)
    up_lots = lots(up_weight)
    cols, pool0, cot0 = call(
        taps_kernel,
        [((TAPS_PAD, 2 * quad_rows, WIDTH), BF16), pool_shape, volume],
        [],
        work,
        taps,
        pooled,
        stacked,
        *from_quad(stacked, devices),
    )
    hidden, down_last = call(
        hidden_kernel,
        [((2 * quad_rows, WIDTH), BF16), spread[2]],
        [],
        2 * work,
        device,
        cols,
        *down_lots,
        *idle(cot0),
    )
    down_spread = (*down_lots[:2], down_last)
    hiddens = (hidden,) + from_quad(hidden, devices)
    act0, up_last = call(
        first_act_kernel,
        [small, spread[2]],
        [],
        work,
        device,
        pool0,
        *up_lots,
        *idle(cot0),
    )
    up_spread = (*up_lots[:2], up_last)
    acts0 = (act0,) + from_quad(act0, devices)
    grads0, *partial = call(
        first_grad_kernel,
        [small] + [volume] * QUAD,
        [columns],
        2 * work,
        device,
        fold,
        *hiddens,
        *acts0,
        *down_spread,
        *idle(cot0, pooled, *up_spread),
    )
    arrived = [from_partner(partial[bits], bits, devices) for bits in range(1, QUAD)]
    (grad_in0,) = call(
        functools.partial(sum_kernel, 1 + QUAD),
        [volume],
        [],
        0,
        cot0,
        partial[0],
        *arrived,
        *idle(grads0, pooled, *up_spread, *down_spread, *hiddens),
    )
    cot1 = lax.ppermute(grad_in0, "loop", [((i + 1) % sections, i) for i in range(sections)])
    act1, pool1 = call(
        second_act_kernel,
        [small, pool_shape],
        [],
        2 * work,
        device,
        pooled,
        cot1,
        *from_quad_by_steps(cot1, devices),
        *up_spread,
        *idle(grads0, *down_spread, *hiddens),
    )
    acts1 = (act1,) + from_quad(act1, devices)
    up_parts = call(
        functools.partial(up_kernel, scale),
        block_outs,
        [wide],
        12 * work,
        device,
        pool0,
        pool1,
        *hiddens,
    )
    *down_parts, grads1 = call(
        functools.partial(down_kernel, scale),
        block_outs + [small],
        [wide],
        2 * work,
        device,
        cols,
        grads0,
        *hiddens,
        *acts1,
    )
    partial = call(
        second_grad_kernel,
        [((2 * CELLS, WIDTH), BF16)] * 2,
        [columns],
        2 * work,
        device,
        fold,
        grads1,
        *down_spread,
    )
    got = from_partner(partial[1], 1, devices)
    own, for_x = call(
        core_sum_kernel, [((CELLS, WIDTH), F32), volume], [], ADD_WORK, partial[0], got
    )
    by_x = from_partner(for_x, 2, devices)
    (grad_in1,) = call(
        functools.partial(sum_kernel, 3), [volume], [], ADD_WORK, cot1, own, by_x
    )

    def after(ring):
        waits = {('down', 0): (partial[0],), ('up', 1): (for_x,), ('up', 2): (grad_in1,)}
        return lambda mark: waits.get((ring, mark), ())

    up_sum, _ = ring_reduce(up_parts, -1, devices, after("up"))
    down_sum, _ = ring_reduce(down_parts, 1, devices, after("down"))

    def owned(total):
        return lax.dynamic_slice(total, (skew, 0), (ROWS, WIDTH))[None]

    return (grad_in1.reshape(inputs1.shape), owned(down_sum), owned(up_sum))


def solution(mesh):
    volume = P("loop", "dp", None, None, None, None)
    rows = P("loop", "dp", None)
    return jax.shard_map(
        local,
        mesh=mesh,
        in_specs=(volume, volume, volume, rows, rows),
        out_specs=(volume, rows, rows),
        check_vma=False,
    )
```

```python
import functools

import jax
import jax.numpy as jnp
import numpy as np
from jax import lax
from jax.experimental import pallas as pl
from jax.experimental.pallas import tpu as pltpu
from jax.sharding import PartitionSpec as P

WIDTH = 384
CELLS = 128
HALF = 16
TAPS = 27
TAPS_PAD = 28
ROWS = 324
ROWS_PAD = 336
CUT = 176
RING = 8
QUAD = 4
LOTS = ((0, 1, 7), (2, 6), (3, 5, 4))
ADD_WORK = 4 * ROWS_PAD * WIDTH
BF16 = jnp.bfloat16
F32 = jnp.float32


class Idle:
    def __init__(self, array):
        self.array = array


def idle(*arrays):
    return [Idle(array) for array in arrays]


def tap_matrices():
    taps = np.zeros((TAPS_PAD * HALF, CELLS), np.float32)
    pooled = np.zeros((TAPS_PAD * HALF, CELLS), np.float32)
    sizes, halves = (4, 8, 4), (2, 4, 2)
    for tap in range(TAPS):
        shift = (tap // 9, tap // 3 % 3, tap % 3)
        for cell in range(CELLS):
            at = (cell // 32, cell // 4 % 8, cell % 4)
            for low in range(HALF):
                coarse = (low // 8, low // 2 % 4, low % 2)
                row = tap * HALF + low
                if all(at[i] == 2 * coarse[i] + shift[i] - 1 for i in range(3)):
                    taps[row, cell] = 1
                if all(
                    0 <= at[i] + shift[i] - 1 < sizes[i]
                    and (at[i] + shift[i] - 1) // 2 == coarse[i]
                    for i in range(3)
                ):
                    pooled[row, cell] = 1
    return taps, pooled


def place_of(device, step):
    block = (((device >> 2) + step) & (RING - 1)) * QUAD + (device & (QUAD - 1))
    tap = (TAPS * block) >> 5
    row = ROWS * block - WIDTH * tap
    return tap, pl.multiple_of((row >> 4) << 4, 16)


def dot(left, right, over_left, over_right):
    return lax.dot_general(
        left, right, (((over_left,), (over_right,)), ((), ())), preferred_element_type=F32
    )


def spread_blocks(device, lot, blocks, spread):
    spread[...] = jnp.zeros_like(spread)
    for at, step in enumerate(LOTS[lot]):
        _, row = place_of(device, step)
        pieces = [blocks[at]]
        if step == RING // 2:
            pieces.append(blocks[at + 1])
        for piece in pieces:
            rows = piece.shape[0]
            spread[at, pl.ds(row, rows), :] = piece[...]
            row = row + rows


def each_part(device, spreads):
    for lot, spread in zip(LOTS, spreads):
        for at, step in enumerate(lot):
            tap, _ = place_of(device, step)
            for part in range(2):
                yield tap + part, spread[at, pl.ds(part * WIDTH, WIDTH), :]


def spread_kernel(lot, device_ref, *refs):
    spread_blocks(device_ref[0], lot, refs[: len(LOTS[lot])], refs[-1])


def taps_kernel(
    taps_ref, pooled_ref, own, by_core, by_x, by_both, cols_ref, pool_ref, cot_ref
):
    cot_ref[...] = own[2]
    for sample, ref in enumerate((own, by_core, by_x, by_both)):
        for kind in range(3):
            matrix = pooled_ref if kind == 2 else taps_ref
            values = dot(matrix[...], ref[kind], 1, 0).astype(BF16)
            values = values.reshape(TAPS_PAD, HALF, WIDTH)
            if kind == 2:
                pool_ref[:, pl.ds(sample * HALF, HALF), :] = values
            else:
                cols_ref[:, pl.ds((kind * QUAD + sample) * HALF, HALF), :] = values


def hidden_kernel(device_ref, cols_ref, first, second, *refs):
    blocks, out, last = refs[:4], refs[-2], refs[-1]
    device = device_ref[0]
    spread_blocks(device, 2, blocks, last)
    total = jnp.zeros(out.shape, F32)
    for tap, weight in each_part(device, (first, second, last)):
        total += dot(cols_ref[tap], weight, 1, 0)
    out[...] = total.astype(BF16)


def act_grad(device, pool_ref, spreads):
    total = jnp.zeros((QUAD * HALF, WIDTH), F32)
    for tap, weight in each_part(device, spreads):
        total += dot(pool_ref[tap], weight, 1, 1)
    return total.astype(BF16)


def first_act_kernel(device_ref, pool_ref, first, second, *refs):
    blocks, out, last = refs[:4], refs[-2], refs[-1]
    device = device_ref[0]
    spread_blocks(device, 2, blocks, last)
    out[...] = act_grad(device, pool_ref, (first, second, last))


def second_act_kernel(device_ref, pooled_ref, *refs):
    sources, spreads, out, pool_ref = refs[:4], refs[4:7], refs[-2], refs[-1]
    for sample, ref in enumerate(sources):
        values = dot(pooled_ref[...], ref[...], 1, 0).astype(BF16)
        pool_ref[:, pl.ds(sample * HALF, HALF), :] = values.reshape(TAPS_PAD, HALF, WIDTH)
    out[...] = act_grad(device_ref[0], pool_ref, spreads)


def quad_total(refs, first_row):
    pieces = []
    for sample in range(QUAD):
        piece = None
        for partner in range(QUAD):
            rows = pl.ds(first_row + (sample ^ partner) * HALF, HALF)
            term = refs[partner][rows, :].astype(F32)
            piece = term if piece is None else piece + term
        pieces.append(piece)
    return jnp.concatenate(pieces, axis=0)


def hidden_grad(hidden, grad):
    sigma = jax.nn.sigmoid(hidden)
    return (grad * sigma * (1.0 + hidden * (1.0 - sigma))).astype(BF16)


def input_grad(device, grads, fold_ref, spreads, columns, outs):
    columns[...] = jnp.zeros_like(columns)
    for tap, weight in each_part(device, spreads):
        values = dot(grads, weight, 1, 1).astype(BF16)
        for sample in range(QUAD):
            columns[sample, tap] = values[sample * HALF : (sample + 1) * HALF]
    for sample in range(QUAD):
        taps = columns[sample].reshape(TAPS_PAD * HALF, WIDTH)
        rows = pl.ds((sample >> 1) * CELLS, CELLS)
        outs[sample & 1][rows, :] = dot(fold_ref[...], taps, 1, 0).astype(BF16)


def first_grad_kernel(device_ref, fold_ref, *refs):
    hidden, grad, spreads = refs[:4], refs[4:8], refs[8:11]
    grad_out, outs, columns = refs[-4], refs[-3:-1], refs[-1]
    grads = hidden_grad(quad_total(hidden, 0), quad_total(grad, 0))
    grad_out[...] = grads
    input_grad(device_ref[0], grads, fold_ref, spreads, columns, outs)


def second_grad_kernel(device_ref, fold_ref, grads_ref, *refs):
    spreads, outs, columns = refs[:3], refs[-3:-1], refs[-1]
    input_grad(device_ref[0], grads_ref[...], fold_ref, spreads, columns, outs)


def core_sum_kernel(kept, got, *refs):
    own, for_x = refs[-2:]
    total = kept[...].astype(F32) + got[...].astype(F32)
    own[...] = total[:CELLS]
    for_x[...] = total[CELLS:].astype(BF16)


def sum_kernel(*refs):
    total = refs[0][...].astype(F32)
    for ref in refs[1:3]:
        total += ref[...].astype(F32)
    refs[-1][...] = total.astype(BF16)


def put_rows(device, step, wide, out, scale):
    _, row = place_of(device, step)
    out[...] = (wide[pl.ds(row, ROWS_PAD), :] * scale).astype(BF16)


def down_kernel(scale, device_ref, cols_ref, first_ref, *refs):
    hidden, grad, outs = refs[:4], refs[4:8], refs[8 : 8 + RING]
    grad_out, wide = refs[8 + RING], refs[9 + RING]
    device = device_ref[0]
    second = hidden_grad(quad_total(hidden, QUAD * HALF), quad_total(grad, 0))
    grad_out[...] = second
    both = jnp.concatenate([first_ref[...], second], axis=0)
    for step in range(RING):
        tap, _ = place_of(device, step)
        for part in range(2):
            wide[step % 2, pl.ds(part * WIDTH, WIDTH), :] = dot(cols_ref[tap + part], both, 0, 0)
        put_rows(device, step, wide.at[step % 2], outs[step], scale)


def up_kernel(scale, device_ref, first_pool, second_pool, *refs):
    hidden, outs, wide = refs[:4], refs[4 : 4 + RING], refs[4 + RING]
    device = device_ref[0]
    rows = QUAD * HALF
    total = jnp.concatenate([quad_total(hidden, 0), quad_total(hidden, rows)], axis=0)
    active = jax.nn.silu(total).astype(BF16)
    for step in range(RING):
        tap, _ = place_of(device, step)
        for part in range(2):
            pools = jnp.concatenate([first_pool[tap + part], second_pool[tap + part]], axis=0)
            wide[step % 2, pl.ds(part * WIDTH, WIDTH), :] = dot(active, pools, 0, 0)
        put_rows(device, step, wide.at[step % 2], outs[step], scale)


def call(kernel, outs, scratch, flops, *operands):
    in_vmem = pl.BlockSpec(memory_space=pltpu.VMEM)

    def place(operand):
        if isinstance(operand, Idle):
            return pl.BlockSpec(memory_space=pl.ANY)
        if operand.dtype == jnp.int32:
            return pl.BlockSpec(memory_space=pltpu.SMEM)
        return in_vmem

    specs = [place(operand) for operand in operands]
    arrays = [o.array if isinstance(o, Idle) else o for o in operands]
    moved = sum(array.size * 2 for array in arrays)
    return pl.pallas_call(
        kernel,
        out_shape=[jax.ShapeDtypeStruct(shape, dtype) for shape, dtype in outs],
        in_specs=specs,
        out_specs=[in_vmem] * len(outs),
        scratch_shapes=[pltpu.VMEM(shape, dtype) for shape, dtype in scratch],
        compiler_params=pltpu.CompilerParams(vmem_limit_bytes=14 * 1024 * 1024),
        cost_estimate=pl.CostEstimate(flops=flops, bytes_accessed=moved, transcendentals=0),
    )(*arrays)


def from_partner(block, bits, devices):
    return lax.ppermute(block, "dp", [(i ^ bits, i) for i in range(devices)])


def from_quad(block, devices):
    return tuple(from_partner(block, bits, devices) for bits in (1, 2, 3))


def from_ring(block, ahead, devices):
    return lax.ppermute(block, "dp", [((i + QUAD * ahead) % devices, i) for i in range(devices)])


def ring_gather(block, devices):
    held = [None] * RING
    held[0] = up = down = block
    for step in range(1, RING // 2):
        held[step] = up = from_ring(up, 1, devices)
        held[RING - step] = down = from_ring(down, -1, devices)
    held[RING // 2] = from_ring(up[:CUT], 1, devices)
    return held + [from_ring(down[CUT:], -1, devices)]


def from_quad_by_steps(block, devices):
    by_x = from_partner(block, 2, devices)
    return from_partner(block, 1, devices), by_x, from_partner(by_x, 1, devices)


def add_kernel(sides, *refs):
    gots, owns, outs = refs[:sides], refs[sides : 2 * sides], refs[-sides:]
    for got, own, out in zip(gots, owns, outs):
        out[...] = (own[...].astype(F32) + got[...].astype(F32)).astype(BF16)


def ring_reduce(blocks, far, devices, after=lambda mark: ()):
    block, near = ((ROWS_PAD, WIDTH), BF16), -far
    far_at, near_at = RING // 2, RING // 2 - 1
    far_sum, near_sum = blocks[far_at], blocks[near_at * near % RING]
    marks = []
    while near_at:
        far_sum = from_ring(far_sum, -far, devices)
        near_sum = from_ring(near_sum, -near, devices)
        far_at, near_at = far_at - 1, near_at - 1
        gots, owns, rest = [far_sum], [blocks[far_at * far % RING]], [blocks[0]]
        if near_at:
            gots.append(near_sum)
            owns.append(blocks[near_at * near % RING])
        else:
            rest.append(near_sum)
        sums = call(
            functools.partial(add_kernel, len(gots)),
            [block] * len(gots),
            [],
            ADD_WORK,
            *gots,
            *owns,
            *idle(*rest, *after(len(marks))),
        )
        far_sum = sums[0]
        if near_at:
            near_sum = sums[1]
        marks.append(far_sum)
    far_sum = from_ring(far_sum, -far, devices)
    return blocks[0].astype(F32) + far_sum.astype(F32) + near_sum.astype(F32), marks


def local(inputs0, inputs1, cotan0, down_weight, up_weight):
    devices = lax.axis_size("dp")
    sections = lax.axis_size("loop")
    index = lax.axis_index("dp")
    device = index.astype(jnp.int32).reshape(1)
    skew = (ROWS * index) % 16
    scale = 1.0 / (2 * devices)
    taps_np, pooled_np = tap_matrices()
    taps, pooled = jnp.asarray(taps_np, BF16), jnp.asarray(pooled_np, BF16)
    fold = jnp.asarray(taps_np.T, BF16)

    def aligned(weight):
        return lax.dynamic_update_slice(jnp.zeros((ROWS_PAD, WIDTH), BF16), weight[0], (skew, 0))

    stacked = jnp.stack(
        [array.reshape(CELLS, WIDTH) for array in (inputs0, inputs1, cotan0)], axis=0
    )
    quad_rows = QUAD * HALF
    spread = [((len(lot), 2 * WIDTH, WIDTH), BF16) for lot in LOTS]
    columns = ((QUAD, TAPS_PAD, HALF, WIDTH), BF16)
    wide = ((2, 2 * WIDTH, WIDTH), F32)
    pool_shape = ((TAPS_PAD, quad_rows, WIDTH), BF16)
    small = ((quad_rows, WIDTH), BF16)
    volume = ((CELLS, WIDTH), BF16)
    pair = ((2 * CELLS, WIDTH), BF16)
    block_outs = [((ROWS_PAD, WIDTH), BF16)] * RING
    work = 2 * quad_rows * 2 * RING * WIDTH * WIDTH

    def lots(weight):
        blocks = ring_gather(aligned(weight), devices)
        early = [blocks[step] for step in LOTS[0]]
        (first,) = call(functools.partial(spread_kernel, 0), [spread[0]], [], 0, device, *early)
        middle = [blocks[step] for step in LOTS[1]]
        (second,) = call(
            functools.partial(spread_kernel, 1), [spread[1]], [], 0, device, *middle, Idle(first)
        )
        return first, second, blocks[3], blocks[5], blocks[4], blocks[RING]

    down_lots = lots(down_weight)
    up_lots = lots(up_weight)
    cols, pool0, cot0 = call(
        taps_kernel,
        [((TAPS_PAD, 2 * quad_rows, WIDTH), BF16), pool_shape, volume],
        [],
        work,
        taps,
        pooled,
        stacked,
        *from_quad(stacked, devices),
    )
    hidden, down_last = call(
        hidden_kernel,
        [((2 * quad_rows, WIDTH), BF16), spread[2]],
        [],
        2 * work,
        device,
        cols,
        *down_lots,
        *idle(cot0),
    )
    down_spread = (*down_lots[:2], down_last)
    hiddens = (hidden,) + from_quad(hidden, devices)
    act0, up_last = call(
        first_act_kernel,
        [small, spread[2]],
        [],
        work,
        device,
        pool0,
        *up_lots,
        *idle(cot0),
    )
    up_spread = (*up_lots[:2], up_last)
    acts0 = (act0,) + from_quad(act0, devices)
    def part_sums(kept, sent):
        parts = [((CELLS, WIDTH), F32), volume]
        got = from_partner(sent, 1, devices)
        own, for_x = call(core_sum_kernel, parts, [], 0, kept, got)
        return own, from_partner(for_x, 2, devices)

    grads0, *partial = call(
        first_grad_kernel,
        [small] + [pair] * 2,
        [columns],
        2 * work,
        device,
        fold,
        *hiddens,
        *acts0,
        *down_spread,
        *idle(cot0, pooled, *up_spread),
    )
    (grad_in0,) = call(
        sum_kernel,
        [volume],
        [],
        0,
        cot0,
        *part_sums(*partial),
        *idle(grads0, pooled, *up_spread, *down_spread, *hiddens),
    )
    cot1 = lax.ppermute(grad_in0, "loop", [((i + 1) % sections, i) for i in range(sections)])
    act1, pool1 = call(
        second_act_kernel,
        [small, pool_shape],
        [],
        2 * work,
        device,
        pooled,
        cot1,
        *from_quad_by_steps(cot1, devices),
        *up_spread,
        *idle(grads0, *down_spread, *hiddens),
    )
    acts1 = (act1,) + from_quad(act1, devices)
    up_parts = call(
        functools.partial(up_kernel, scale),
        block_outs,
        [wide],
        2 * work,
        device,
        pool0,
        pool1,
        *hiddens,
    )
    *down_parts, grads1 = call(
        functools.partial(down_kernel, scale),
        block_outs + [small],
        [wide],
        2 * work,
        device,
        cols,
        grads0,
        *hiddens,
        *acts1,
    )
    partial = call(
        second_grad_kernel,
        [pair] * 2,
        [columns],
        2 * work,
        device,
        fold,
        grads1,
        *down_spread,
    )
    (grad_in1,) = call(sum_kernel, [volume], [], 0, cot1, *part_sums(*partial))

    def after(ring):
        waits = {('down', 0): (partial[0],), ('up', 2): (grad_in1,)}
        return lambda mark: waits.get((ring, mark), ())

    up_sum, _ = ring_reduce(up_parts, -1, devices, after("up"))
    down_sum, _ = ring_reduce(down_parts, 1, devices, after("down"))

    def owned(total):
        return lax.dynamic_slice(total, (skew, 0), (ROWS, WIDTH))[None]

    return (grad_in1.reshape(inputs1.shape), owned(down_sum), owned(up_sum))


def solution(mesh):
    volume = P("loop", "dp", None, None, None, None)
    rows = P("loop", "dp", None)
    return jax.shard_map(
        local,
        mesh=mesh,
        in_specs=(volume, volume, volume, rows, rows),
        out_specs=(volume, rows, rows),
        check_vma=False,
    )
```
